512 devices in a mesh: wide: 64 (over z_lo, x, core), narrow: 8 (over z_hi, y).
Axes of the slice: x: 4, y: 4, z: 16 (z_hi: 2, z_lo: 8; z = z_hi * 8 + z_lo), core: 2. Of those that a mesh axis runs over, the one named last changes fastest.
Arguments:
- tokens: bfloat16 [384, 12288], P('wide', 'narrow'), may hold values from -6 to 6
- up_weight: bfloat16 [12288, 49152], P('narrow', 'wide'), may hold values from -0.0546875 to 0.0546875
- down_weight: bfloat16 [49152, 12288], P('wide', 'narrow'), may hold values from -0.02734375 to 0.02734375
- partner: int32 [384], P('wide'), may hold values from 0 to 383, as said below
- spans: int32 [64, 2], P('wide'), may hold values from 1 to 5, as said below
Outputs:
- blended: bfloat16 [384, 12288], P('wide', 'narrow')
The draws below stay inside these ranges and needn't reach their ends.
Inputs may be any that keep to these rules, and one draw needn't show every extreme that they name: Row r of block b has partner b' * 6 + j with some row j, where b' = b - 1 if r < spans[b, 0] and b > 0, b' = b + 1 if r >= spans[b, 1] and b < 63; every other token is its own partner. spans[b, 0] lies in 1 to 2 and spans[b, 1] in 4 to 5.
All inputs are finite; a program needn't handle non-finite values.
Results may differ from the reference program's by a relative error of at most 0.0049.
Values may be sent and summed in bfloat16 or wider, within the bound.
A program may use at most 64 MiB of HBM per device.

```python
import jax
import jax.numpy as jnp

D = 12288
FF = 49152
TOK_DEV = 6
TOKENS = 384


def intersection_bounds(key):
    third = TOK_DEV // 3
    offsets = jax.random.randint(jax.random.fold_in(key, 11), (2,), 0, third)
    block_index = jnp.arange(TOKENS // TOK_DEV, dtype=jnp.int32)
    lower_edge = 1 + (block_index + offsets[0]) % third
    upper_edge = TOK_DEV - 1 - (block_index * 3 + offsets[1]) % third
    return (lower_edge, upper_edge)


def draw_spans(key, part):
    lower_edge, upper_edge = intersection_bounds(key)
    return jnp.stack([lower_edge, upper_edge], axis=1).astype(jnp.int32)


def draw_partner(key, part):
    lower_edge, upper_edge = intersection_bounds(key)
    key = jax.random.fold_in(key, 5)
    row_index = jnp.arange(TOKENS, dtype=jnp.int32)
    block_index = row_index // TOK_DEV
    position = row_index % TOK_DEV
    choose_row = jax.random.randint(key, (TOKENS,), 0, TOK_DEV)
    last_block = TOKENS // TOK_DEV - 1
    to_left = (position < lower_edge[block_index]) & (block_index > 0)
    to_right = (position >= upper_edge[block_index]) & (block_index < last_block)
    result = jnp.where(to_left, (block_index - 1) * TOK_DEV + choose_row, jnp.where(to_right, (block_index + 1) * TOK_DEV + choose_row, row_index))
    return result.astype(jnp.int32)


def level_of(stream_key, shape, split, low, top_value):
    def one(axis_at, parts):
        draws = jax.random.uniform(jax.random.fold_in(jax.random.fold_in(stream_key, 6), axis_at), (parts,), jnp.float32, low / len(split), top_value / len(split))
        return jnp.repeat(jnp.exp(draws), shape[axis_at] // parts).reshape((-1,) + (1,) * (len(shape) - axis_at - 1))

    level = one(*split[0])
    for cut in split[1:]:
        level = level * one(*cut)
    return level


def gaussian(stream_key, dims, scale, limit, split=(), kind=jnp.bfloat16):
    drawn = scale * jax.random.normal(stream_key, dims, jnp.float32)
    if split:
        drawn = drawn * level_of(stream_key, dims, split, -0.22, 0.18)
    return jnp.clip(drawn, -limit, limit).astype(kind)


def setup_inputs(seed: int = 0) -> dict:
    key_list = jax.random.split(jax.random.key(seed), 6)
    tokens = gaussian(key_list[0], (TOKENS, D), 1.0, 6.0, ((0, 64), (1, 8)))
    up_weight = gaussian(key_list[1], (D, FF), D ** -0.5, 0.0546875, ((0, 8), (1, 64)))
    down_weight = gaussian(key_list[2], (FF, D), FF ** -0.5, 0.02734375, ((0, 64), (1, 8)))
    partner = draw_partner(jax.random.fold_in(key_list[5], 71), 0)
    spans = draw_spans(jax.random.fold_in(key_list[5], 71), 0)
    return {"tokens": tokens, "up_weight": up_weight, "down_weight": down_weight, "partner": partner, "spans": spans}


def blend_weights(spans, row_count):
    position = jnp.arange(row_count, dtype=jnp.int32)[None, :]
    lower_edge = spans[:, 0:1]
    upper_edge = spans[:, 1:2]
    from_left = jnp.where(position < lower_edge,
                          jnp.float32(0.5) * (lower_edge - position).astype(jnp.float32) / lower_edge.astype(jnp.float32),
                          jnp.float32(0.0))
    from_right = jnp.where(position >= upper_edge,
                           jnp.float32(0.5) * (position - upper_edge + 1).astype(jnp.float32) / (row_count - upper_edge).astype(jnp.float32),
                           jnp.float32(0.0))
    return (from_left + from_right).reshape(-1)


def reference(tokens, up_weight, down_weight, partner, spans):
    preact = jnp.dot(tokens, up_weight, preferred_element_type=jnp.float32)
    hidden = jax.nn.gelu(preact, approximate=True).astype(jnp.bfloat16)
    summed = jnp.dot(hidden, down_weight, preferred_element_type=jnp.float32)
    share = blend_weights(spans, TOK_DEV)
    blended = summed + share[:, None] * (summed[partner] - summed)
    return blended.astype(jnp.bfloat16)
```

```python
import jax
import jax.numpy as jnp
from jax import lax
from jax.experimental import pallas as pl
from jax.experimental.pallas import tpu as pltpu
from jax.sharding import PartitionSpec as P

MESH = pl.DeviceIdType.MESH
BF16 = jnp.bfloat16
F32 = jnp.float32

NZ, NX, NC, NY = 8, 4, 2, 4
ROWS = 6
SLAB = NZ * ROWS
GROUPS = NC * NX
TOKENS = GROUPS * SLAB
DM = 1536
FF = 768
GA = 2
WA = DM // GA
KB = 3
WB = FF // KB
JD = 3
WD = DM // JD
YR = TOKENS // NY


def steps(values, size, count):
    total = jnp.zeros_like(values)
    for k in range(1, count):
        total = total + jnp.where(values >= size * k, 1, 0)
    return total


def onehot(condition):
    return jnp.where(condition, 1.0, 0.0).astype(BF16)


def dot(a, b):
    return jnp.dot(a, b, preferred_element_type=F32)


def token_of(place):
    group = steps(place, SLAB, GROUPS)
    inside = place - SLAB * group
    z = steps(inside, ROWS, NZ)
    core = jnp.where(group >= NX, 1, 0)
    block = (z * NX + (group - NX * core)) * NC + core
    return block, ROWS * block + inside - ROWS * z


def kernel(
    tok_ref, partner_ref, spans_ref, up_hbm, down_hbm, out_ref,
    up, down, zbuf, g0, g1, p1, mix, ysend, yrecv, ysum, hsend, hrecv, hid, p2,
    csend, crecv, xsend, xrecv, xown, zsend, zrecv,
    wsem, az_s, az_r, ax_s, ax_r, ac_s, ac_r, by_s, by_r, bh_s, bh_r, cy_s, cy_r,
    dc_s, dc_r, dx_s, dx_r, dz_s, dz_r,
):
    w = lax.axis_index("wide")
    n = lax.axis_index("narrow")
    z, x, c = w // 8, (w // 2) % 4, w % 2
    half, y = n // 4, n % 4
    g = (g0, g1)

    def z_peer(d):
        return (((z + d) % NZ * NX + x) * NC + c, n)

    def x_peer(d):
        return ((z * NX + (x + d) % NX) * NC + c, n)

    def y_peer(d):
        return (w, half * NY + (y + d) % NY)

    core_peer = ((z * NX + x) * NC + 1 - c, n)
    half_peer = (w, (1 - half) * NY + y)

    def remote(src, dst, send, recv, peer):
        return pltpu.make_async_remote_copy(
            src_ref=src, dst_ref=dst, send_sem=send, recv_sem=recv, device_id=peer, device_id_type=MESH
        )

    sent = []

    def start(copy):
        copy.start()
        sent.append(copy)

    up_copy = pltpu.make_async_copy(up_hbm, up, wsem.at[0])
    down_copy = pltpu.make_async_copy(down_hbm, down, wsem.at[1])
    up_copy.start()
    down_copy.start()

    barrier = pltpu.get_barrier_semaphore()
    peers = [half_peer]
    peers += [z_peer(d) for d in range(1, NZ)]
    peers += [y_peer(d) for d in range(1, NY)]
    peers += [x_peer(d) for d in range(1, NX)]
    peers += [core_peer]
    for peer in peers:
        pl.semaphore_signal(barrier, inc=1, device_id=peer, device_id_type=MESH)

    tokens = tok_ref[...].astype(F32)
    tokens = jnp.concatenate([tokens, jnp.zeros((2, DM), F32)], axis=0)
    for i in range(GA):
        left = tokens[:, i * WA : i * WA + WA // 2]
        right = tokens[:, i * WA + WA // 2 : (i + 1) * WA]
        plane = jnp.concatenate([left, right], axis=0)
        if i == GA - 1:
            row = lax.broadcasted_iota(jnp.int32, (16, WA // 2), 0)
            lane = lax.broadcasted_iota(jnp.int32, (16, WA // 2), 1)
            lower = jnp.full((16, WA // 2), spans_ref[0, 0], jnp.int32).astype(F32)
            upper = jnp.full((16, WA // 2), spans_ref[0, 1], jnp.int32).astype(F32)
            for r in range(ROWS):
                relative = partner_ref[r] - ROWS * (w - 1)
                relative = jnp.full((16, WA // 2), relative, jnp.int32).astype(F32)
                share = jnp.where(lower > r, 0.5 * (lower - r) / lower, 0.0) + jnp.where(
                    upper <= r, 0.5 * (r - upper + 1.0) / (ROWS - upper), 0.0
                )
                here = row == ROWS + r // 3
                plane = jnp.where(here & (lane == 128 * (r % 3)), relative, plane)
                plane = jnp.where(here & (lane == 128 * (r % 3) + 1), share, plane)
        zbuf[i, z] = plane.astype(BF16)

    pl.semaphore_wait(barrier, len(peers))

    for i in range(GA):
        for d in (7, 1, 6, 2, 5, 3, 4):
            mine = zbuf.at[i, z]
            start(remote(mine, mine, az_s.at[i, d], az_r.at[i, d], z_peer(d)))

    m_at = lax.broadcasted_iota(jnp.int32, (SLAB, NZ * 16), 0)
    q_at = lax.broadcasted_iota(jnp.int32, (SLAB, NZ * 16), 1)
    m_z = steps(m_at, ROWS, NZ)
    m_r = m_at - ROWS * m_z
    pick_left = onehot(q_at == 16 * m_z + m_r)
    pick_right = onehot(q_at == 16 * m_z + m_r + 8)
    m_third = jnp.where(m_r >= 3, 1, 0)
    pick_info = [
        onehot((q_at == 16 * m_z + ROWS + m_third) & (m_r - 3 * m_third == t)) for t in range(3)
    ]

    group = c * NX + x
    for i in range(GA):
        for d in range(1, NZ):
            slot = zbuf.at[i, (z + NZ - d) % NZ]
            remote(slot, slot, az_s.at[i, d], az_r.at[i, d], z_peer(d)).wait_recv()
        planes = zbuf[i].reshape(NZ * 16, WA // 2)
        g[i][group, :, 0 : WA // 2] = dot(pick_left, planes).astype(BF16)
        g[i][group, :, WA // 2 : WA] = dot(pick_right, planes).astype(BF16)
        if i == GA - 1:
            info = dot(pick_info[0], planes[:, 0:128])
            info = info + dot(pick_info[1], planes[:, 128:256])
            info = info + dot(pick_info[2], planes[:, 256:384])
            g[i][group, :, WA : WA + 128] = info.astype(BF16)
        slab = g[i].at[group]
        for d in (2, 1, 3):
            start(remote(slab, slab, ax_s.at[i, d], ax_r.at[i, d], x_peer(d)))
        start(remote(slab, slab, ac_s.at[i, 0], ac_r.at[i, 0], core_peer))

    up_copy.wait()
    for i in range(GA):
        for d in (1, 3, 2):
            slab = g[i].at[c * NX + (x + NX - d) % NX]
            remote(slab, slab, ax_s.at[i, d], ax_r.at[i, d], x_peer(d)).wait_recv()
            start(remote(slab, slab, ac_s.at[i, d], ac_r.at[i, d], core_peer))
        for d in (0, 1, 3, 2):
            slab = g[i].at[(1 - c) * NX + (x + NX - d) % NX]
            remote(slab, slab, ac_s.at[i, d], ac_r.at[i, d], core_peer).wait_recv()
        a = g[i][:, :, 0:WA].reshape(TOKENS, WA)
        rows = pl.ds(i * WA, WA)
        for k in range(KB):
            part = dot(a, up[rows, k * WB : (k + 1) * WB]).reshape(NY, YR, WB)
            if i == 0:
                p1[k] = part
            else:
                part = part + p1[k]
                p1[k] = part
                ysend[k] = part.astype(BF16)
                for d in (2, 1, 3):
                    start(
                        remote(
                            ysend.at[k, (y + d) % NY], yrecv.at[k, d], by_s.at[k, d], by_r.at[k, d], y_peer(d)
                        )
                    )

    info = g1[:, :, WA : WA + 128].reshape(TOKENS, 128).astype(F32)
    block, _ = token_of(lax.broadcasted_iota(jnp.int32, (TOKENS, 1), 0))
    partner = (ROWS * (block - 1)).astype(F32) + info[:, 0:1]
    share = info[:, 1:2]
    _, token = token_of(lax.broadcasted_iota(jnp.int32, (1, TOKENS), 1))
    at = lax.broadcasted_iota(jnp.int32, (TOKENS, TOKENS), 0)
    to = lax.broadcasted_iota(jnp.int32, (TOKENS, TOKENS), 1)
    matrix = jnp.where(at == to, 1.0 - share, 0.0) + jnp.where(token.astype(F32) == partner, share, 0.0)
    mix[...] = matrix.astype(BF16)

    for k in range(KB):
        total = p1[k, y]
        for d in (1, 3, 2):
            remote(yrecv.at[k, d], yrecv.at[k, d], by_s.at[k, d], by_r.at[k, d], y_peer(d)).wait_recv()
            total = total + yrecv[k, d].astype(F32)
        ysum[k] = total
        hsend[k] = total.astype(BF16)
        start(remote(hsend.at[k], hrecv.at[k], bh_s.at[k], bh_r.at[k], half_peer))
    for k in range(KB):
        remote(hsend.at[k], hrecv.at[k], bh_s.at[k], bh_r.at[k], half_peer).wait_recv()
        preact = ysum[k] + hrecv[k].astype(F32)
        hid[k, y] = jax.nn.gelu(preact, approximate=True).astype(BF16)
        mine = hid.at[k, y]
        for d in (2, 1, 3):
            start(remote(mine, mine, cy_s.at[k, d], cy_r.at[k, d], y_peer(d)))

    down_copy.wait()
    for k in range(KB):
        for d in (1, 3, 2):
            slot = hid.at[k, (y + NY - d) % NY]
            remote(slot, slot, cy_s.at[k, d], cy_r.at[k, d], y_peer(d)).wait_recv()
        hidden = dot(mix[...], hid[k].reshape(TOKENS, WB)).astype(BF16)
        rows = pl.ds(k * WB, WB)
        if k < KB - 1:
            part = dot(hidden, down[rows, :])
            if k > 0:
                part = part + p2[...].reshape(TOKENS, DM)
            p2[...] = part.reshape(NC, TOKENS // NC, DM)
        else:
            for j in range(JD):
                cols = pl.ds(j * WD, WD)
                part = dot(hidden, down[rows, j * WD : (j + 1) * WD])
                p2[:, :, cols] = p2[:, :, cols] + part.reshape(NC, TOKENS // NC, WD)
                csend[j] = p2[1 - c, :, cols].astype(BF16)
                start(remote(csend.at[j], crecv.at[j], dc_s.at[j], dc_r.at[j], core_peer))

    for j in range(JD):
        remote(csend.at[j], crecv.at[j], dc_s.at[j], dc_r.at[j], core_peer).wait_recv()
        total = p2[c, :, pl.ds(j * WD, WD)] + crecv[j].astype(F32)
        total = total.reshape(NX, SLAB, WD)
        xown[j] = total
        xsend[j] = total.astype(BF16)
        for d in (2, 1, 3):
            start(remote(xsend.at[j, (x + d) % NX], xrecv.at[j, d], dx_s.at[j, d], dx_r.at[j, d], x_peer(d)))
    p_at = lax.broadcasted_iota(jnp.int32, (NZ * 16, SLAB), 0)
    s_at = lax.broadcasted_iota(jnp.int32, (NZ * 16, SLAB), 1)
    p_z = steps(p_at, 16, NZ)
    p_r = p_at - 16 * p_z
    put_left = onehot((s_at == ROWS * p_z + p_r) & (p_r < ROWS))
    put_right = onehot((s_at == ROWS * p_z + p_r - 8) & (p_r >= 8) & (p_r < 8 + ROWS))
    for j in range(JD):
        total = xown[j, x]
        for d in (1, 3, 2):
            remote(xrecv.at[j, d], xrecv.at[j, d], dx_s.at[j, d], dx_r.at[j, d], x_peer(d)).wait_recv()
            total = total + xrecv[j, d].astype(F32)
        total = total.astype(BF16)
        planes = dot(put_left, total[:, 0 : WD // 2]) + dot(put_right, total[:, WD // 2 : WD])
        zsend[j] = planes.reshape(NZ, 16, WD // 2).astype(BF16)
        for d in (7, 1, 6, 2, 5, 3, 4):
            start(remote(zsend.at[j, (z + d) % NZ], zrecv.at[j, d], dz_s.at[j, d], dz_r.at[j, d], z_peer(d)))
    for j in range(JD):
        total = zsend[j, z].astype(F32)
        for d in (1, 7, 2, 6, 3, 5, 4):
            remote(zrecv.at[j, d], zrecv.at[j, d], dz_s.at[j, d], dz_r.at[j, d], z_peer(d)).wait_recv()
            total = total + zrecv[j, d].astype(F32)
        out_ref[:, j * WD : j * WD + WD // 2] = total[0:ROWS].astype(BF16)
        out_ref[:, j * WD + WD // 2 : (j + 1) * WD] = total[8 : 8 + ROWS].astype(BF16)

    for copy in sent:
        copy.wait_send()


def body(tokens, up_weight, down_weight, partner, spans):
    dma = pltpu.SemaphoreType.DMA
    vmem = pltpu.VMEM
    return pl.pallas_call(
        kernel,
        out_shape=jax.ShapeDtypeStruct((ROWS, DM), BF16),
        in_specs=[
            pl.BlockSpec(memory_space=vmem),
            pl.BlockSpec(memory_space=pltpu.SMEM),
            pl.BlockSpec(memory_space=pltpu.SMEM),
            pl.BlockSpec(memory_space=pl.ANY),
            pl.BlockSpec(memory_space=pl.ANY),
        ],
        out_specs=pl.BlockSpec(memory_space=vmem),
        scratch_shapes=[
            vmem((DM, FF), BF16),
            vmem((FF, DM), BF16),
            vmem((GA, NZ, 16, WA // 2), BF16),
            vmem((GROUPS, SLAB, WA), BF16),
            vmem((GROUPS, SLAB, WA + 128), BF16),
            vmem((KB, NY, YR, WB), F32),
            vmem((TOKENS, TOKENS), BF16),
            vmem((KB, NY, YR, WB), BF16),
            vmem((KB, NY, YR, WB), BF16),
            vmem((KB, YR, WB), F32),
            vmem((KB, YR, WB), BF16),
            vmem((KB, YR, WB), BF16),
            vmem((KB, NY, YR, WB), BF16),
            vmem((NC, TOKENS // NC, DM), F32),
            vmem((JD, TOKENS // NC, WD), BF16),
            vmem((JD, TOKENS // NC, WD), BF16),
            vmem((JD, NX, SLAB, WD), BF16),
            vmem((JD, NX, SLAB, WD), BF16),
            vmem((JD, NX, SLAB, WD), F32),
            vmem((JD, NZ, 16, WD // 2), BF16),
            vmem((JD, NZ, 16, WD // 2), BF16),
            dma((2,)),
            dma((GA, NZ)), dma((GA, NZ)),
            dma((GA, NX)), dma((GA, NX)),
            dma((GA, NX)), dma((GA, NX)),
            dma((KB, NY)), dma((KB, NY)),
            dma((KB,)), dma((KB,)),
            dma((KB, NY)), dma((KB, NY)),
            dma((JD,)), dma((JD,)),
            dma((JD, NX)), dma((JD, NX)),
            dma((JD, NZ)), dma((JD, NZ)),
        ],
        compiler_params=pltpu.CompilerParams(
            collective_id=0, has_side_effects=True, vmem_limit_bytes=48 << 20
        ),
    )(tokens, partner, spans, up_weight, down_weight)


def solution(mesh):
    placed = (
        P("wide", "narrow"),
        P("narrow", "wide"),
        P("wide", "narrow"),
        P("wide"),
        P("wide", None),
    )
    return jax.shard_map(
        body, mesh=mesh, in_specs=placed, out_specs=P("wide", "narrow"), check_vma=False
    )
```

```python
import jax
import jax.numpy as jnp
from jax import lax
from jax.experimental import pallas as pl
from jax.experimental.pallas import tpu as pltpu
from jax.sharding import PartitionSpec as P

MESH = pl.DeviceIdType.MESH
BF16 = jnp.bfloat16
F32 = jnp.float32

NZ, NX, NC, NY = 8, 4, 2, 4
ROWS = 6
SLAB = NZ * ROWS
GROUPS = NC * NX
TOKENS = GROUPS * SLAB
DM = 1536
FF = 768
GATED = {"bh": 3}
Z_SEND = (4, 5, 6, 7, 3, 2, 1)
Z_RECV = (1, 2, 3, 4, 5, 6, 7)
KB = 6
WB = FF // KB
YR = TOKENS // NY


def steps(values, size, count):
    total = jnp.zeros_like(values)
    for k in range(1, count):
        total = total + jnp.where(values >= size * k, 1, 0)
    return total


def onehot(condition):
    return jnp.where(condition, 1.0, 0.0).astype(BF16)


def dot(a, b):
    return jnp.dot(a, b, preferred_element_type=F32)


def token_of(place):
    group = steps(place, SLAB, GROUPS)
    inside = place - SLAB * group
    z = steps(inside, ROWS, NZ)
    core = jnp.where(group >= NX, 1, 0)
    block = (z * NX + (group - NX * core)) * NC + core
    return block, ROWS * block + inside - ROWS * z


def kernel(
    tok_hbm, partner_hbm, spans_hbm, up_hbm, down_hbm, out_ref,
    tok_ref, partner_ref, spans_ref, up, down, planes, g, p1, mix, ysend, yrecv, ysum, hsend, hrecv, hid, p2,
    crecv, xsend, xrecv, xown, zsend, zrecv,
    wsem, az_s, az_r, ax_s, ax_r, ac_s, ac_r, by_s, by_r, bh_s, bh_r, cy_s, cy_r,
    dc_s, dc_r, dx_s, dx_r, dz_s, dz_r,
):
    w = lax.axis_index("wide")
    n = lax.axis_index("narrow")
    z, x, c = w // 8, (w // 2) % 4, w % 2
    half, y = n // 4, n % 4

    def z_at(step):
        bits = (z // 4, z // 2 % 2, z % 2)
        flip = (step // 4, step // 2 % 2, step % 2)
        high, middle, low = ((1 - b) if f else b for b, f in zip(bits, flip))
        return 4 * high + 2 * middle + low

    def z_peer(step):
        return ((z_at(step) * NX + x) * NC + c, n)

    def x_peer(d):
        return ((z * NX + (x + d) % NX) * NC + c, n)

    def y_peer(d):
        return (w, half * NY + (y + d) % NY)

    core_peer = ((z * NX + x) * NC + 1 - c, n)
    half_peer = (w, (1 - half) * NY + y)

    def remote(src, dst, send, recv, peer):
        return pltpu.make_async_remote_copy(
            src_ref=src, dst_ref=dst, send_sem=send, recv_sem=recv, device_id=peer, device_id_type=MESH
        )

    sent = []
    flying = {}

    def start(copy, phase=None):
        copy.start()
        if phase in GATED:
            flying[phase][-1].append(copy)
        else:
            sent.append(copy)

    def gate(phase):
        if phase in GATED:
            chunks = flying.setdefault(phase, [])
            if len(chunks) == GATED[phase]:
                for copy in chunks.pop(0):
                    copy.wait_send()
            chunks.append([])

    up_copy = pltpu.make_async_copy(up_hbm, up, wsem.at[0])
    down_copy = pltpu.make_async_copy(down_hbm, down, wsem.at[1])
    tok_copy = pltpu.make_async_copy(tok_hbm, tok_ref, wsem.at[2])
    partner_copy = pltpu.make_async_copy(partner_hbm, partner_ref, wsem.at[3])
    spans_copy = pltpu.make_async_copy(spans_hbm, spans_ref, wsem.at[4])
    tok_copy.start()
    partner_copy.start()
    spans_copy.start()
    up_copy.start()
    down_copy.start()

    barrier = pltpu.get_barrier_semaphore()
    peers = [half_peer]
    peers += [z_peer(d) for d in range(1, NZ)]
    peers += [y_peer(d) for d in range(1, NY)]
    peers += [x_peer(d) for d in range(1, NX)]
    peers += [core_peer]
    for peer in peers:
        pl.semaphore_signal(barrier, inc=1, device_id=peer, device_id_type=MESH)

    tok_copy.wait()
    partner_copy.wait()
    spans_copy.wait()
    tokens = tok_ref[...].astype(F32)
    row = lax.broadcasted_iota(jnp.int32, (ROWS, 128), 0)
    lane = lax.broadcasted_iota(jnp.int32, (ROWS, 128), 1)
    lower = jnp.full((ROWS, 128), spans_ref[0, 0], jnp.int32).astype(F32)
    upper = jnp.full((ROWS, 128), spans_ref[0, 1], jnp.int32).astype(F32)
    place = row.astype(F32)
    relative = jnp.zeros((ROWS, 128), F32)
    for r in range(ROWS):
        value = jnp.full((ROWS, 128), partner_ref[r] - ROWS * (w - 1), jnp.int32).astype(F32)
        relative = jnp.where(row == r, value, relative)
    share = jnp.where(lower > place, 0.5 * (lower - place) / lower, 0.0) + jnp.where(
        upper <= place, 0.5 * (place - upper + 1.0) / (ROWS - upper), 0.0
    )
    info = jnp.where(lane == 0, relative, jnp.where(lane == 1, share, 0.0))
    t10, t11 = tokens[:, 1280:1408], tokens[:, 1408:1536]
    tails = (
        (t10[0:4],),
        (t10[4:6], t11[0:2]),
        (t11[2:6],),
        (info[0:4],),
        (info[4:6], jnp.zeros((2, 128), F32)),
    )
    group = c * NX + x
    for j in range(5):
        main = (tokens[:, j * 128 : (j + 1) * 128], tokens[:, 640 + j * 128 : 768 + j * 128])
        tile = jnp.concatenate(main + tails[j], axis=0)
        planes[group, z, :, j * 128 : (j + 1) * 128] = tile.astype(BF16)

    pl.semaphore_wait(barrier, len(peers))

    def plane(column, step):
        return planes.at[c * NX + column, z_at(step)]

    for step in Z_SEND:
        mine = plane(x, 0)
        start(remote(mine, mine, az_s.at[step], az_r.at[step], z_peer(step)))

    m_at = lax.broadcasted_iota(jnp.int32, (SLAB, NZ * 16), 0)
    q_at = lax.broadcasted_iota(jnp.int32, (SLAB, NZ * 16), 1)
    m_z = steps(m_at, ROWS, NZ)
    m_r = m_at - ROWS * m_z
    q_r = q_at - 16 * m_z
    pick_low = onehot(q_r == m_r)
    pick_high = onehot(q_r == m_r + 6)
    pick_a = onehot((m_r < 4) & (q_r == m_r + 12))
    pick_b = onehot((m_r >= 4) & (q_r == m_r + 8))
    pick_c = onehot((m_r < 2) & (q_r == m_r + 14))
    pick_d = onehot((m_r >= 2) & (q_r == m_r + 10))

    def spread(step):
        if step:
            mine = plane(x, step)
            remote(mine, mine, az_s.at[step], az_r.at[step], z_peer(step)).wait_recv()
        mine = plane(x, step)
        for d in (2, 1, 3):
            start(remote(mine, mine, ax_s.at[step, d], ax_r.at[step, d], x_peer(d)))

    for step in (0, *Z_RECV):
        spread(step)

    for d in (0, 1, 3, 2):
        column = (x + NX - d) % NX
        if d:
            for step in (0, *Z_RECV):
                there = plane(column, step)
                remote(there, there, ax_s.at[step, d], ax_r.at[step, d], x_peer(d)).wait_recv()
        at = c * NX + column
        whole = planes[at].reshape(NZ * 16, 640)
        g[at, :, 0:640] = dot(pick_low, whole).astype(BF16)
        g[at, :, 640:1280] = dot(pick_high, whole).astype(BF16)
        tail = dot(pick_a, whole[:, 0:128]) + dot(pick_b, whole[:, 128:256])
        g[at, :, 1280:1408] = tail.astype(BF16)
        tail = dot(pick_c, whole[:, 128:256]) + dot(pick_d, whole[:, 256:384])
        g[at, :, 1408:1536] = tail.astype(BF16)
        tail = dot(pick_a, whole[:, 384:512]) + dot(pick_b, whole[:, 512:640])
        g[at, :, 1536:1664] = tail.astype(BF16)
        slab = g.at[at]
        start(remote(slab, slab, ac_s.at[d], ac_r.at[d], core_peer))

    up_copy.wait()
    for i in range(2):
        core = c if i == 0 else 1 - c
        if i:
            for d in (0, 1, 3, 2):
                slab = g.at[(1 - c) * NX + (x + NX - d) % NX]
                remote(slab, slab, ac_s.at[d], ac_r.at[d], core_peer).wait_recv()
        a = g[pl.ds(core * NX, NX), :, 0:DM].reshape(TOKENS // NC, DM)
        for k in range(KB):
            part = dot(a, up[:, k * WB : (k + 1) * WB]).reshape(2, YR, WB)
            p1[k, pl.ds(2 * core, 2)] = part
            ysend[k, pl.ds(2 * core, 2)] = part.astype(BF16)
            if i:
                gate("by")
                for d in (2, 1, 3):
                    mine = ysend.at[k, (y + d) % NY]
                    start(remote(mine, yrecv.at[k, d], by_s.at[k, d], by_r.at[k, d], y_peer(d)), "by")

    info = g[:, :, DM : DM + 128].reshape(TOKENS, 128).astype(F32)
    block, _ = token_of(lax.broadcasted_iota(jnp.int32, (TOKENS, 1), 0))
    partner = (ROWS * (block - 1)).astype(F32) + info[:, 0:1]
    share = info[:, 1:2]
    _, token = token_of(lax.broadcasted_iota(jnp.int32, (1, TOKENS), 1))
    at = lax.broadcasted_iota(jnp.int32, (TOKENS, TOKENS), 0)
    to = lax.broadcasted_iota(jnp.int32, (TOKENS, TOKENS), 1)
    matrix = jnp.where(at == to, 1.0 - share, 0.0) + jnp.where(token.astype(F32) == partner, share, 0.0)
    mix[...] = matrix.astype(BF16).reshape(NC, TOKENS // NC, TOKENS)

    for k in range(KB):
        total = p1[k, y]
        for d in (1, 3, 2):
            remote(yrecv.at[k, d], yrecv.at[k, d], by_s.at[k, d], by_r.at[k, d], y_peer(d)).wait_recv()
            total = total + yrecv[k, d].astype(F32)
        ysum[k] = total
        hsend[k] = total.astype(BF16)
        gate("bh")
        start(remote(hsend.at[k], hrecv.at[k], bh_s.at[k], bh_r.at[k], half_peer), "bh")
    for k in range(KB):
        remote(hsend.at[k], hrecv.at[k], bh_s.at[k], bh_r.at[k], half_peer).wait_recv()
        preact = ysum[k] + hrecv[k].astype(F32)
        hid[k, y] = jax.nn.gelu(preact, approximate=True).astype(BF16)
        mine = hid.at[k, y]
        gate("cy")
        for d in (2, 1, 3):
            start(remote(mine, mine, cy_s.at[k, d], cy_r.at[k, d], y_peer(d)), "cy")

    down_copy.wait()
    for k in range(KB):
        for d in (1, 3, 2):
            slot = hid.at[k, (y + NY - d) % NY]
            remote(slot, slot, cy_s.at[k, d], cy_r.at[k, d], y_peer(d)).wait_recv()
        hidden = hid[k].reshape(TOKENS, WB)
        rows = pl.ds(k * WB, WB)
        if k < KB - 1:
            hidden = dot(mix[...].reshape(TOKENS, TOKENS), hidden).astype(BF16)
            part = dot(hidden, down[rows, :]).reshape(p2.shape)
            p2[...] = part if k == 0 else part + p2[...]
        else:
            for core in (1 - c, c):
                part = dot(dot(mix[core], hidden).astype(BF16), down[rows, :])
                p2[core] = p2[core] + part.reshape(NX, 2, SLAB // 2, DM)
                if core is not c:
                    for far in (1, 0):
                        mine = p2.at[1 - c, :, z_at(4 * far) // 4]
                        start(remote(mine, crecv.at[far], dc_s.at[far], dc_r.at[far], core_peer))

    p_at = lax.broadcasted_iota(jnp.int32, (NX * 64, NX * SLAB // 2), 0)
    s_at = lax.broadcasted_iota(jnp.int32, (NX * 64, NX * SLAB // 2), 1)
    p_block = steps(p_at, 16, NX * 4)
    p_row = p_at - 16 * p_block
    s_row = s_at - ROWS * p_block
    put_low = onehot((p_row < 6) & (s_row == p_row))
    put_high = onehot((p_row >= 6) & (p_row < 12) & (s_row == p_row - 6))
    put_a = onehot((p_row >= 12) & (s_row == p_row - 12))
    put_b = onehot((p_row >= 12) & (p_row < 14) & (s_row == p_row - 8))
    put_c = onehot((p_row >= 14) & (s_row == p_row - 14))
    put_d = onehot((p_row >= 12) & (s_row == p_row - 10))

    def packed(rows, j):
        tile = dot(put_low, rows[:, j * 128 : (j + 1) * 128])
        tile = tile + dot(put_high, rows[:, 640 + j * 128 : 768 + j * 128])
        t10, t11 = rows[:, 1280:1408], rows[:, 1408:1536]
        if j == 0:
            tile = tile + dot(put_a, t10)
        if j == 1:
            tile = tile + dot(put_b, t10) + dot(put_c, t11)
        if j == 2:
            tile = tile + dot(put_d, t11)
        return tile.reshape(NX, 4, 16, 128)

    order = ((7, 6, 5, 4), (3, 2, 1, 0))
    for far in (1, 0):
        mine = p2.at[1 - c, :, z_at(4 * far) // 4]
        remote(mine, crecv.at[far], dc_s.at[far], dc_r.at[far], core_peer).wait_recv()
        total = (p2[c, :, z_at(4 * far) // 4] + crecv[far]).reshape(NX * SLAB // 2, DM)
        first = total.astype(BF16)
        for j in range(5):
            xsend[far, :, :, :, j * 128 : (j + 1) * 128] = packed(first, j).astype(BF16)
        for step in order[1 - far]:
            for d in (2, 1, 3):
                mine = xsend.at[far, (x + d) % NX, z_at(step) % 4]
                start(remote(mine, xrecv.at[step, d], dx_s.at[step, d], dx_r.at[step, d], x_peer(d)))
        rest = (total - first.astype(F32)).astype(BF16)
        for j in range(5):
            xown[far, :, :, :, j * 128 : (j + 1) * 128] = packed(rest, j)
    for step in (*order[0], *order[1]):
        far, at = step // 4, z_at(step) % 4
        total = xown[far, x, at] + xsend[far, x, at].astype(F32)
        for d in (1, 3, 2):
            there = xrecv.at[step, d]
            remote(there, there, dx_s.at[step, d], dx_r.at[step, d], x_peer(d)).wait_recv()
            total = total + xrecv[step, d].astype(F32)
        if step:
            zsend[step] = total.astype(BF16)
            start(remote(zsend.at[step], zrecv.at[step], dz_s.at[step], dz_r.at[step], z_peer(step)))
    for step in (1, 2, 3, 4, 5, 6, 7):
        remote(zsend.at[step], zrecv.at[step], dz_s.at[step], dz_r.at[step], z_peer(step)).wait_recv()
        total = total + zrecv[step].astype(F32)
    for j in range(5):
        tile = total[:, j * 128 : (j + 1) * 128]
        out_ref[:, j * 128 : (j + 1) * 128] = tile[0:6].astype(BF16)
        out_ref[:, 640 + j * 128 : 768 + j * 128] = tile[6:12].astype(BF16)
    t10 = (total[12:16, 0:128], total[12:14, 128:256])
    t11 = (total[14:16, 128:256], total[12:16, 256:384])
    out_ref[:, 1280:1408] = jnp.concatenate(t10, axis=0).astype(BF16)
    out_ref[:, 1408:1536] = jnp.concatenate(t11, axis=0).astype(BF16)

    for chunks in ([sent], *flying.values()):
        for copies in chunks:
            for copy in copies:
                copy.wait_send()


def body(tokens, up_weight, down_weight, partner, spans):
    dma = pltpu.SemaphoreType.DMA
    vmem = pltpu.VMEM
    return pl.pallas_call(
        kernel,
        out_shape=jax.ShapeDtypeStruct((ROWS, DM), BF16),
        in_specs=[pl.BlockSpec(memory_space=pltpu.HBM)] * 5,
        out_specs=pl.BlockSpec(memory_space=vmem),
        scratch_shapes=[
            vmem((ROWS, DM), BF16),
            pltpu.SMEM((ROWS,), jnp.int32),
            pltpu.SMEM((1, 2), jnp.int32),
            vmem((DM, FF), BF16),
            vmem((FF, DM), BF16),
            vmem((GROUPS, NZ, 16, 640), BF16),
            vmem((GROUPS, SLAB, DM + 128), BF16),
            vmem((KB, NY, YR, WB), F32),
            vmem((NC, TOKENS // NC, TOKENS), BF16),
            vmem((KB, NY, YR, WB), BF16),
            vmem((KB, NY, YR, WB), BF16),
            vmem((KB, YR, WB), F32),
            vmem((KB, YR, WB), BF16),
            vmem((KB, YR, WB), BF16),
            vmem((KB, NY, YR, WB), BF16),
            vmem((NC, NX, 2, SLAB // 2, DM), F32),
            vmem((2, NX, SLAB // 2, DM), F32),
            vmem((2, NX, 4, 16, 640), BF16),
            vmem((NZ, NX, 16, 640), BF16),
            vmem((2, NX, 4, 16, 640), F32),
            vmem((NZ, 16, 640), BF16),
            vmem((NZ, 16, 640), BF16),
            dma((5,)),
            dma((NZ,)), dma((NZ,)),
            dma((NZ, NX)), dma((NZ, NX)),
            dma((NX,)), dma((NX,)),
            dma((KB, NY)), dma((KB, NY)),
            dma((KB,)), dma((KB,)),
            dma((KB, NY)), dma((KB, NY)),
            dma((2,)), dma((2,)),
            dma((NZ, NX)), dma((NZ, NX)),
            dma((NZ,)), dma((NZ,)),
        ],
        compiler_params=pltpu.CompilerParams(
            collective_id=0, has_side_effects=True, vmem_limit_bytes=60 << 20
        ),
    )(tokens, partner, spans, up_weight, down_weight)


def solution(mesh):
    placed = (
        P("wide", "narrow"),
        P("narrow", "wide"),
        P("wide", "narrow"),
        P("wide"),
        P("wide", None),
    )
    return jax.shard_map(
        body, mesh=mesh, in_specs=placed, out_specs=P("wide", "narrow"), check_vma=False
    )
```

```python
import jax
import jax.numpy as jnp
from jax import lax
from jax.experimental import pallas as pl
from jax.experimental.pallas import tpu as pltpu
from jax.sharding import PartitionSpec as P

MESH = pl.DeviceIdType.MESH
BF16 = jnp.bfloat16
F32 = jnp.float32

NZ, NX, NC, NY = 8, 4, 2, 4
ROWS = 6
SLAB = NZ // 2 * ROWS
PART = NX * SLAB
HALF = NC * PART
TOKENS = 2 * HALF
DM = 1536
FF = 768
GATED = {}
EARLY = 4
Z_SEND = (1, 2, 3, 4, 5, 6, 7)
KB = 3
WB = FF // KB
YR = HALF // NY


def steps(values, size, count):
    total = jnp.zeros_like(values)
    for k in range(1, count):
        total = total + jnp.where(values >= size * k, 1, 0)
    return total


def onehot(condition):
    return jnp.where(condition, 1.0, 0.0).astype(BF16)


def dot(a, b):
    return jnp.dot(a, b, preferred_element_type=F32)


def token_of(place, z_high):
    group = steps(place, SLAB, TOKENS // SLAB)
    inside = place - SLAB * group
    low = steps(inside, ROWS, NZ // 2)
    far = jnp.where(group >= NC * NX, 1, 0)
    core = jnp.where(group - NC * NX * far >= NX, 1, 0)
    column = group - NC * NX * far - NX * core
    z = (NZ // 2) * (z_high + far - 2 * z_high * far) + low
    block = (z * NX + column) * NC + core
    return block, ROWS * block + inside - ROWS * low


def kernel(
    tok_hbm, partner_hbm, spans_hbm, up_hbm, down_hbm, out_ref,
    tok_ref, partner_ref, spans_ref, up, down, planes, g, p1, mix, ysend, yrecv, ysum, hsend, hrecv, hid, p2,
    crecv, xsend, xrecv, xown, zsend, zrecv,
    wsem, az_s, az_r, ax_s, ax_r, ac_s, ac_r, by_s, by_r, bh_s, bh_r, cy_s, cy_r,
    dc_s, dc_r, dx_s, dx_r, dz_s, dz_r,
):
    w = lax.axis_index("wide")
    n = lax.axis_index("narrow")
    z, x, c = w // 8, (w // 2) % 4, w % 2
    half, y = n // 4, n % 4

    def z_at(step):
        bits = (z // 4, z // 2 % 2, z % 2)
        flip = (step // 4, step // 2 % 2, step % 2)
        high, middle, low = ((1 - b) if f else b for b, f in zip(bits, flip))
        return 4 * high + 2 * middle + low

    def z_peer(step):
        return ((z_at(step) * NX + x) * NC + c, n)

    def x_peer(d):
        return ((z * NX + (x + d) % NX) * NC + c, n)

    def y_peer(d):
        return (w, half * NY + (y + d) % NY)

    core_peer = ((z * NX + x) * NC + 1 - c, n)
    half_peer = (w, (1 - half) * NY + y)

    def remote(src, dst, send, recv, peer):
        return pltpu.make_async_remote_copy(
            src_ref=src, dst_ref=dst, send_sem=send, recv_sem=recv, device_id=peer, device_id_type=MESH
        )

    sent = []
    flying = {}

    def start(copy, phase=None):
        copy.start()
        if phase in GATED:
            flying[phase][-1].append(copy)
        else:
            sent.append(copy)

    def gate(phase):
        if phase in GATED:
            chunks = flying.setdefault(phase, [])
            if len(chunks) == GATED[phase]:
                for copy in chunks.pop(0):
                    copy.wait_send()
            chunks.append([])

    up_copy = pltpu.make_async_copy(up_hbm, up, wsem.at[0])
    down_copy = pltpu.make_async_copy(down_hbm, down, wsem.at[1])
    tok_copy = pltpu.make_async_copy(tok_hbm, tok_ref, wsem.at[2])
    partner_copy = pltpu.make_async_copy(partner_hbm, partner_ref, wsem.at[3])
    spans_copy = pltpu.make_async_copy(spans_hbm, spans_ref, wsem.at[4])
    tok_copy.start()
    partner_copy.start()
    spans_copy.start()
    up_copy.start()
    down_copy.start()

    barrier = pltpu.get_barrier_semaphore()
    peers = [half_peer]
    peers += [z_peer(d) for d in range(1, NZ)]
    peers += [y_peer(d) for d in range(1, NY)]
    peers += [x_peer(d) for d in range(1, NX)]
    peers += [core_peer]
    for peer in peers:
        pl.semaphore_signal(barrier, inc=1, device_id=peer, device_id_type=MESH)

    tok_copy.wait()
    partner_copy.wait()
    spans_copy.wait()
    tokens = tok_ref[...].astype(F32)
    row = lax.broadcasted_iota(jnp.int32, (ROWS, 128), 0)
    lane = lax.broadcasted_iota(jnp.int32, (ROWS, 128), 1)
    lower = jnp.full((ROWS, 128), spans_ref[0, 0], jnp.int32).astype(F32)
    upper = jnp.full((ROWS, 128), spans_ref[0, 1], jnp.int32).astype(F32)
    place = row.astype(F32)
    relative = jnp.zeros((ROWS, 128), F32)
    for r in range(ROWS):
        value = jnp.full((ROWS, 128), partner_ref[r] - ROWS * (w - 1), jnp.int32).astype(F32)
        relative = jnp.where(row == r, value, relative)
    share = jnp.where(lower > place, 0.5 * (lower - place) / lower, 0.0) + jnp.where(
        upper <= place, 0.5 * (place - upper + 1.0) / (ROWS - upper), 0.0
    )
    info = jnp.where(lane == 0, relative, jnp.where(lane == 1, share, 0.0))
    t10, t11 = tokens[:, 1280:1408], tokens[:, 1408:1536]
    tails = (
        (t10[0:4],),
        (t10[4:6], t11[0:2]),
        (t11[2:6],),
        (info[0:4],),
        (info[4:6], jnp.zeros((2, 128), F32)),
    )
    for j in range(5):
        main = (tokens[:, j * 128 : (j + 1) * 128], tokens[:, 640 + j * 128 : 768 + j * 128])
        tile = jnp.concatenate(main + tails[j], axis=0)
        planes[0, c, x, z % 4, :, j * 128 : (j + 1) * 128] = tile.astype(BF16)

    pl.semaphore_wait(barrier, len(peers))

    def plane(column, step):
        return planes.at[step // 4, c, column, z_at(step) % 4]

    for step in Z_SEND:
        there = planes.at[step // 4, c, x, z % 4]
        start(remote(plane(x, 0), there, az_s.at[step], az_r.at[step], z_peer(step)))

    def spread(step):
        mine = plane(x, step)
        if step:
            remote(mine, mine, az_s.at[step], az_r.at[step], z_peer(step)).wait_recv()
        for d in (2, 1, 3):
            start(remote(mine, mine, ax_s.at[step, d], ax_r.at[step, d], x_peer(d)))

    m_at = lax.broadcasted_iota(jnp.int32, (PART, PART * 16 // ROWS), 0)
    q_at = lax.broadcasted_iota(jnp.int32, (PART, PART * 16 // ROWS), 1)
    m_block = steps(m_at, ROWS, PART // ROWS)
    m_r = m_at - ROWS * m_block
    q_r = q_at - 16 * m_block
    pick_low = onehot(q_r == m_r)
    pick_high = onehot(q_r == m_r + 6)
    pick_a = onehot((m_r < 4) & (q_r == m_r + 12))
    pick_b = onehot((m_r >= 4) & (q_r == m_r + 8))
    pick_c = onehot((m_r < 2) & (q_r == m_r + 14))
    pick_d = onehot((m_r >= 2) & (q_r == m_r + 10))

    def unpack(far):
        for d in (1, 3, 2):
            for step in range(4 * far, 4 * far + 4):
                there = plane((x + NX - d) % NX, step)
                remote(there, there, ax_s.at[step, d], ax_r.at[step, d], x_peer(d)).wait_recv()
        whole = planes[far, c].reshape(PART * 16 // ROWS, 640)
        g[far, c, :, 0:640] = dot(pick_low, whole).astype(BF16)
        g[far, c, :, 640:1280] = dot(pick_high, whole).astype(BF16)
        tail = dot(pick_a, whole[:, 0:128]) + dot(pick_b, whole[:, 128:256])
        g[far, c, :, 1280:1408] = tail.astype(BF16)
        tail = dot(pick_c, whole[:, 128:256]) + dot(pick_d, whole[:, 256:384])
        g[far, c, :, 1408:1536] = tail.astype(BF16)
        tail = dot(pick_a, whole[:, 384:512]) + dot(pick_b, whole[:, 512:640])
        g[far, c, :, 1536:1664] = tail.astype(BF16)
        mine = g.at[far, c]
        start(remote(mine, mine, ac_s.at[far], ac_r.at[far], core_peer))

    def project(far):
        there = g.at[far, 1 - c]
        remote(there, there, ac_s.at[far], ac_r.at[far], core_peer).wait_recv()
        a = g[far, :, :, 0:DM].reshape(HALF, DM)
        for k in range(KB):
            part = dot(a, up[:, k * WB : (k + 1) * WB]).reshape(NY, YR, WB)
            p1[far, k] = part
            ysend[far, k] = part.astype(BF16)
            gate("by")
            for d in (2, 1, 3):
                mine = ysend.at[far, k, (y + d) % NY]
                to = yrecv.at[far, k, d]
                start(remote(mine, to, by_s.at[far, k, d], by_r.at[far, k, d], y_peer(d)), "by")

    def exchange(far):
        for k in range(KB):
            total = p1[far, k, y]
            for d in (1, 3, 2):
                there = yrecv.at[far, k, d]
                remote(there, there, by_s.at[far, k, d], by_r.at[far, k, d], y_peer(d)).wait_recv()
                total = total + yrecv[far, k, d].astype(F32)
            ysum[far, k] = total
            hsend[far, k] = total.astype(BF16)
            gate("bh")
            mine = hsend.at[far, k]
            start(remote(mine, hrecv.at[far, k], bh_s.at[far, k], bh_r.at[far, k], half_peer), "bh")

    for step in range(EARLY):
        spread(step)
    unpack(0)
    for step in range(EARLY, NZ):
        spread(step)
    up_copy.wait()
    project(0)
    unpack(1)
    exchange(0)
    project(1)

    info = g[:, :, :, DM : DM + 128].reshape(TOKENS, 128).astype(F32)
    block, _ = token_of(lax.broadcasted_iota(jnp.int32, (TOKENS, 1), 0), z // 4)
    partner = (ROWS * (block - 1)).astype(F32) + info[:, 0:1]
    share = info[:, 1:2]
    _, token = token_of(lax.broadcasted_iota(jnp.int32, (1, TOKENS), 1), z // 4)
    at = lax.broadcasted_iota(jnp.int32, (TOKENS, TOKENS), 0)
    to = lax.broadcasted_iota(jnp.int32, (TOKENS, TOKENS), 1)
    matrix = jnp.where(at == to, 1.0 - share, 0.0) + jnp.where(token.astype(F32) == partner, share, 0.0)
    mix[...] = matrix.astype(BF16).reshape(mix.shape)

    exchange(1)
    for far in range(2):
        for k in range(KB):
            there = hrecv.at[far, k]
            remote(there, there, bh_s.at[far, k], bh_r.at[far, k], half_peer).wait_recv()
            preact = ysum[far, k] + hrecv[far, k].astype(F32)
            hid[k, far, y] = jax.nn.gelu(preact, approximate=True).astype(BF16)
            mine = hid.at[k, far, y]
            gate("cy")
            for d in (2, 1, 3):
                start(remote(mine, mine, cy_s.at[far, k, d], cy_r.at[far, k, d], y_peer(d)), "cy")

    down_copy.wait()
    for k in range(KB):
        for far in range(2):
            for d in (1, 3, 2):
                there = hid.at[k, far, (y + NY - d) % NY]
                remote(there, there, cy_s.at[far, k, d], cy_r.at[far, k, d], y_peer(d)).wait_recv()
        hidden = hid[k].reshape(TOKENS, WB)
        rows = pl.ds(k * WB, WB)
        if k < KB - 1:
            hidden = dot(mix[...].reshape(TOKENS, TOKENS), hidden).astype(BF16)
            part = dot(hidden, down[rows, :]).reshape(p2.shape)
            p2[...] = part if k == 0 else part + p2[...]
        else:
            for core in (1 - c, c):
                mixed = dot(mix[:, core].reshape(HALF, TOKENS), hidden).astype(BF16)
                part = dot(mixed, down[rows, :])
                p2[:, core] = p2[:, core] + part.reshape(2, NX, SLAB, DM)
                if core is not c:
                    for far in (1, 0):
                        mine = p2.at[far, 1 - c]
                        start(remote(mine, crecv.at[far], dc_s.at[far], dc_r.at[far], core_peer))

    p_at = lax.broadcasted_iota(jnp.int32, (NX * 64, PART), 0)
    s_at = lax.broadcasted_iota(jnp.int32, (NX * 64, PART), 1)
    p_block = steps(p_at, 16, NX * 4)
    p_row = p_at - 16 * p_block
    s_row = s_at - ROWS * p_block
    put_low = onehot((p_row < 6) & (s_row == p_row))
    put_high = onehot((p_row >= 6) & (p_row < 12) & (s_row == p_row - 6))
    put_a = onehot((p_row >= 12) & (s_row == p_row - 12))
    put_b = onehot((p_row >= 12) & (p_row < 14) & (s_row == p_row - 8))
    put_c = onehot((p_row >= 14) & (s_row == p_row - 14))
    put_d = onehot((p_row >= 12) & (s_row == p_row - 10))

    def packed(rows, j):
        tile = dot(put_low, rows[:, j * 128 : (j + 1) * 128])
        tile = tile + dot(put_high, rows[:, 640 + j * 128 : 768 + j * 128])
        t10, t11 = rows[:, 1280:1408], rows[:, 1408:1536]
        if j == 0:
            tile = tile + dot(put_a, t10)
        if j == 1:
            tile = tile + dot(put_b, t10) + dot(put_c, t11)
        if j == 2:
            tile = tile + dot(put_d, t11)
        return tile.reshape(NX, 4, 16, 128)

    order = ((7, 6, 5, 4), (3, 2, 1, 0))
    for far in (1, 0):
        mine = p2.at[far, 1 - c]
        remote(mine, crecv.at[far], dc_s.at[far], dc_r.at[far], core_peer).wait_recv()
        total = (p2[far, c] + crecv[far]).reshape(PART, DM)
        first = total.astype(BF16)
        for j in range(5):
            xsend[far, :, :, :, j * 128 : (j + 1) * 128] = packed(first, j).astype(BF16)
        for step in order[1 - far]:
            for d in (2, 1, 3):
                mine = xsend.at[far, (x + d) % NX, z_at(step) % 4]
                start(remote(mine, xrecv.at[step, d], dx_s.at[step, d], dx_r.at[step, d], x_peer(d)))
        rest = (total - first.astype(F32)).astype(BF16)
        for j in range(5):
            xown[far, :, :, :, j * 128 : (j + 1) * 128] = packed(rest, j)
    for step in (*order[0], *order[1]):
        far, at = step // 4, z_at(step) % 4
        total = xown[far, x, at] + xsend[far, x, at].astype(F32)
        for d in (1, 3, 2):
            there = xrecv.at[step, d]
            remote(there, there, dx_s.at[step, d], dx_r.at[step, d], x_peer(d)).wait_recv()
            total = total + xrecv[step, d].astype(F32)
        if step:
            zsend[step] = total.astype(BF16)
            start(remote(zsend.at[step], zrecv.at[step], dz_s.at[step], dz_r.at[step], z_peer(step)))
    for step in (1, 2, 3, 4, 5, 6, 7):
        remote(zsend.at[step], zrecv.at[step], dz_s.at[step], dz_r.at[step], z_peer(step)).wait_recv()
        total = total + zrecv[step].astype(F32)
    for j in range(5):
        tile = total[:, j * 128 : (j + 1) * 128]
        out_ref[:, j * 128 : (j + 1) * 128] = tile[0:6].astype(BF16)
        out_ref[:, 640 + j * 128 : 768 + j * 128] = tile[6:12].astype(BF16)
    t10 = (total[12:16, 0:128], total[12:14, 128:256])
    t11 = (total[14:16, 128:256], total[12:16, 256:384])
    out_ref[:, 1280:1408] = jnp.concatenate(t10, axis=0).astype(BF16)
    out_ref[:, 1408:1536] = jnp.concatenate(t11, axis=0).astype(BF16)

    for chunks in ([sent], *flying.values()):
        for copies in chunks:
            for copy in copies:
                copy.wait_send()


def body(tokens, up_weight, down_weight, partner, spans):
    dma = pltpu.SemaphoreType.DMA
    vmem = pltpu.VMEM
    return pl.pallas_call(
        kernel,
        out_shape=jax.ShapeDtypeStruct((ROWS, DM), BF16),
        in_specs=[pl.BlockSpec(memory_space=pltpu.HBM)] * 5,
        out_specs=pl.BlockSpec(memory_space=vmem),
        scratch_shapes=[
            vmem((ROWS, DM), BF16),
            pltpu.SMEM((ROWS,), jnp.int32),
            pltpu.SMEM((1, 2), jnp.int32),
            vmem((DM, FF), BF16),
            vmem((FF, DM), BF16),
            vmem((2, NC, NX, NZ // 2, 16, 640), BF16),
            vmem((2, NC, PART, DM + 128), BF16),
            vmem((2, KB, NY, YR, WB), F32),
            vmem((2, NC, PART, TOKENS), BF16),
            vmem((2, KB, NY, YR, WB), BF16),
            vmem((2, KB, NY, YR, WB), BF16),
            vmem((2, KB, YR, WB), F32),
            vmem((2, KB, YR, WB), BF16),
            vmem((2, KB, YR, WB), BF16),
            vmem((KB, 2, NY, YR, WB), BF16),
            vmem((2, NC, NX, SLAB, DM), F32),
            vmem((2, NX, SLAB, DM), F32),
            vmem((2, NX, 4, 16, 640), BF16),
            vmem((NZ, NX, 16, 640), BF16),
            vmem((2, NX, 4, 16, 640), F32),
            vmem((NZ, 16, 640), BF16),
            vmem((NZ, 16, 640), BF16),
            dma((5,)),
            dma((NZ,)), dma((NZ,)),
            dma((NZ, NX)), dma((NZ, NX)),
            dma((2,)), dma((2,)),
            dma((2, KB, NY)), dma((2, KB, NY)),
            dma((2, KB)), dma((2, KB)),
            dma((2, KB, NY)), dma((2, KB, NY)),
            dma((2,)), dma((2,)),
            dma((NZ, NX)), dma((NZ, NX)),
            dma((NZ,)), dma((NZ,)),
        ],
        compiler_params=pltpu.CompilerParams(
            collective_id=0, has_side_effects=True, vmem_limit_bytes=60 << 20
        ),
    )(tokens, partner, spans, up_weight, down_weight)


def solution(mesh):
    placed = (
        P("wide", "narrow"),
        P("narrow", "wide"),
        P("wide", "narrow"),
        P("wide"),
        P("wide", None),
    )
    return jax.shard_map(
        body, mesh=mesh, in_specs=placed, out_specs=P("wide", "narrow"), check_vma=False
    )
```

```python
import jax
import jax.numpy as jnp
from jax import lax
from jax.experimental import pallas as pl
from jax.experimental.pallas import tpu as pltpu
from jax.sharding import PartitionSpec as P

MESH = pl.DeviceIdType.MESH
BF16 = jnp.bfloat16
F32 = jnp.float32

NZ, NX, NC, NY = 8, 4, 2, 4
ROWS = 6
SLAB = NZ // 2 * ROWS
PART = NX * SLAB
HALF = NC * PART
TOKENS = 2 * HALF
DM = 1536
FF = 768
GATED = {}
EARLY = 4
Z_SEND = (1, 2, 3, 4, 5, 6, 7)
KB = 3
WB = FF // KB
YR = HALF // NY


def steps(values, size, count):
    total = jnp.zeros_like(values)
    for k in range(1, count):
        total = total + jnp.where(values >= size * k, 1, 0)
    return total


def onehot(condition):
    return jnp.where(condition, 1.0, 0.0).astype(BF16)


def dot(a, b):
    return jnp.dot(a, b, preferred_element_type=F32)


def token_of(place, z_high):
    group = steps(place, SLAB, TOKENS // SLAB)
    inside = place - SLAB * group
    low = steps(inside, ROWS, NZ // 2)
    far = jnp.where(group >= NC * NX, 1, 0)
    core = jnp.where(group - NC * NX * far >= NX, 1, 0)
    column = group - NC * NX * far - NX * core
    z = (NZ // 2) * (z_high + far - 2 * z_high * far) + low
    block = (z * NX + column) * NC + core
    return block, ROWS * block + inside - ROWS * low


def kernel(
    tok_hbm, partner_hbm, spans_hbm, up_hbm, down_hbm, out_ref,
    tok_ref, partner_ref, spans_ref, up, down, planes, g, p1, mix, ysend, yrecv, ysum, hsend, hrecv, hid, p2,
    crecv, xsend, xrecv, xown, zsend, zrecv,
    wsem, az_s, az_r, ax_s, ax_r, ac_s, ac_r, by_s, by_r, bh_s, bh_r, cy_s, cy_r,
    dc_s, dc_r, dx_s, dx_r, dz_s, dz_r,
):
    w = lax.axis_index("wide")
    n = lax.axis_index("narrow")
    z, x, c = w // 8, (w // 2) % 4, w % 2
    half, y = n // 4, n % 4

    def z_at(step):
        bits = (z // 4, z // 2 % 2, z % 2)
        flip = (step // 4, step // 2 % 2, step % 2)
        high, middle, low = ((1 - b) if f else b for b, f in zip(bits, flip))
        return 4 * high + 2 * middle + low

    def z_peer(step):
        return ((z_at(step) * NX + x) * NC + c, n)

    def x_peer(d):
        return ((z * NX + (x + d) % NX) * NC + c, n)

    def y_peer(d):
        return (w, half * NY + (y + d) % NY)

    core_peer = ((z * NX + x) * NC + 1 - c, n)
    half_peer = (w, (1 - half) * NY + y)

    def remote(src, dst, send, recv, peer):
        return pltpu.make_async_remote_copy(
            src_ref=src, dst_ref=dst, send_sem=send, recv_sem=recv, device_id=peer, device_id_type=MESH
        )

    sent = []
    flying = {}

    def start(copy, phase=None):
        copy.start()
        if phase in GATED:
            flying[phase][-1].append(copy)
        else:
            sent.append(copy)

    def gate(phase):
        if phase in GATED:
            chunks = flying.setdefault(phase, [])
            if len(chunks) == GATED[phase]:
                for copy in chunks.pop(0):
                    copy.wait_send()
            chunks.append([])

    up_copy = pltpu.make_async_copy(up_hbm, up, wsem.at[0])
    down_copy = pltpu.make_async_copy(down_hbm, down, wsem.at[1])
    tok_copy = pltpu.make_async_copy(tok_hbm, tok_ref, wsem.at[2])
    partner_copy = pltpu.make_async_copy(partner_hbm, partner_ref, wsem.at[3])
    spans_copy = pltpu.make_async_copy(spans_hbm, spans_ref, wsem.at[4])
    tok_copy.start()
    partner_copy.start()
    spans_copy.start()
    up_copy.start()
    down_copy.start()

    barrier = pltpu.get_barrier_semaphore()
    peers = [half_peer]
    peers += [z_peer(d) for d in range(1, NZ)]
    peers += [y_peer(d) for d in range(1, NY)]
    peers += [x_peer(d) for d in range(1, NX)]
    peers += [core_peer]
    for peer in peers:
        pl.semaphore_signal(barrier, inc=1, device_id=peer, device_id_type=MESH)

    tok_copy.wait()
    partner_copy.wait()
    spans_copy.wait()
    tokens = tok_ref[...].astype(F32)
    row = lax.broadcasted_iota(jnp.int32, (ROWS, 128), 0)
    lane = lax.broadcasted_iota(jnp.int32, (ROWS, 128), 1)
    lower = jnp.full((ROWS, 128), spans_ref[0, 0], jnp.int32).astype(F32)
    upper = jnp.full((ROWS, 128), spans_ref[0, 1], jnp.int32).astype(F32)
    place = row.astype(F32)
    relative = jnp.zeros((ROWS, 128), F32)
    for r in range(ROWS):
        value = jnp.full((ROWS, 128), partner_ref[r] - ROWS * (w - 1), jnp.int32).astype(F32)
        relative = jnp.where(row == r, value, relative)
    share = jnp.where(lower > place, 0.5 * (lower - place) / lower, 0.0) + jnp.where(
        upper <= place, 0.5 * (place - upper + 1.0) / (ROWS - upper), 0.0
    )
    info = jnp.where(lane == 0, relative, jnp.where(lane == 1, share, 0.0))
    t10, t11 = tokens[:, 1280:1408], tokens[:, 1408:1536]
    tails = (
        (t10[0:4],),
        (t10[4:6], t11[0:2]),
        (t11[2:6],),
        (info[0:4],),
        (info[4:6], jnp.zeros((2, 128), F32)),
    )
    for j in range(5):
        main = (tokens[:, j * 128 : (j + 1) * 128], tokens[:, 640 + j * 128 : 768 + j * 128])
        tile = jnp.concatenate(main + tails[j], axis=0)
        planes[0, c, x, z % 4, :, j * 128 : (j + 1) * 128] = tile.astype(BF16)

    pl.semaphore_wait(barrier, len(peers))

    def plane(column, step):
        return planes.at[step // 4, c, column, z_at(step) % 4]

    for step in Z_SEND:
        there = planes.at[step // 4, c, x, z % 4]
        start(remote(plane(x, 0), there, az_s.at[step], az_r.at[step], z_peer(step)))

    def spread(step):
        mine = plane(x, step)
        if step:
            remote(mine, mine, az_s.at[step], az_r.at[step], z_peer(step)).wait_recv()
        for d in (2, 1, 3):
            start(remote(mine, mine, ax_s.at[step, d], ax_r.at[step, d], x_peer(d)))

    m_at = lax.broadcasted_iota(jnp.int32, (PART, PART * 16 // ROWS), 0)
    q_at = lax.broadcasted_iota(jnp.int32, (PART, PART * 16 // ROWS), 1)
    m_block = steps(m_at, ROWS, PART // ROWS)
    m_r = m_at - ROWS * m_block
    q_r = q_at - 16 * m_block
    picks = jnp.concatenate(
        (
            onehot(q_r == m_r),
            onehot(q_r == m_r + 6),
            onehot((m_r < 4) & (q_r == m_r + 12)),
            onehot((m_r >= 4) & (q_r == m_r + 8)),
            onehot((m_r < 2) & (q_r == m_r + 14)),
            onehot((m_r >= 2) & (q_r == m_r + 10)),
        ),
        axis=0,
    )

    def unpack(far):
        for d in (1, 3, 2):
            for step in range(4 * far, 4 * far + 4):
                there = plane((x + NX - d) % NX, step)
                remote(there, there, ax_s.at[step, d], ax_r.at[step, d], x_peer(d)).wait_recv()
        whole = planes[far, c].reshape(PART * 16 // ROWS, 640)
        low, high, first, second, third, fourth = dot(picks, whole).reshape(6, PART, 640)
        g[far, c, :, 0:640] = low.astype(BF16)
        g[far, c, :, 640:1280] = high.astype(BF16)
        g[far, c, :, 1280:1408] = (first[:, 0:128] + second[:, 128:256]).astype(BF16)
        g[far, c, :, 1408:1536] = (third[:, 128:256] + fourth[:, 256:384]).astype(BF16)
        g[far, c, :, 1536:1664] = (first[:, 384:512] + second[:, 512:640]).astype(BF16)
        mine = g.at[far, c]
        start(remote(mine, mine, ac_s.at[far], ac_r.at[far], core_peer))

    def project(far):
        there = g.at[far, 1 - c]
        remote(there, there, ac_s.at[far], ac_r.at[far], core_peer).wait_recv()
        a = g[far, :, :, 0:DM].reshape(HALF, DM)
        for k in range(KB):
            part = dot(a, up[:, k * WB : (k + 1) * WB]).reshape(NY, YR, WB)
            p1[far, k] = part
            ysend[far, k] = part.astype(BF16)
            gate("by")
            for d in (2, 1, 3):
                mine = ysend.at[far, k, (y + d) % NY]
                to = yrecv.at[far, k, d]
                start(remote(mine, to, by_s.at[far, k, d], by_r.at[far, k, d], y_peer(d)), "by")

    def exchange(far):
        for k in range(KB):
            total = p1[far, k, y]
            for d in (1, 3, 2):
                there = yrecv.at[far, k, d]
                remote(there, there, by_s.at[far, k, d], by_r.at[far, k, d], y_peer(d)).wait_recv()
                total = total + yrecv[far, k, d].astype(F32)
            ysum[far, k] = total
            hsend[far, k] = total.astype(BF16)
            gate("bh")
            mine = hsend.at[far, k]
            start(remote(mine, hrecv.at[far, k], bh_s.at[far, k], bh_r.at[far, k], half_peer), "bh")

    for step in range(EARLY):
        spread(step)
    unpack(0)
    for step in range(EARLY, NZ):
        spread(step)
    up_copy.wait()
    project(0)
    unpack(1)
    exchange(0)
    project(1)

    info = g[:, :, :, DM : DM + 128].reshape(TOKENS, 128).astype(F32)
    block, _ = token_of(lax.broadcasted_iota(jnp.int32, (TOKENS, 1), 0), z // 4)
    partner = (ROWS * (block - 1)).astype(F32) + info[:, 0:1]
    share = info[:, 1:2]
    _, token = token_of(lax.broadcasted_iota(jnp.int32, (1, TOKENS), 1), z // 4)
    at = lax.broadcasted_iota(jnp.int32, (TOKENS, TOKENS), 0)
    to = lax.broadcasted_iota(jnp.int32, (TOKENS, TOKENS), 1)
    matrix = jnp.where(at == to, 1.0 - share, 0.0) + jnp.where(token.astype(F32) == partner, share, 0.0)
    mix[...] = matrix.astype(BF16).reshape(mix.shape)

    exchange(1)
    for far in range(2):
        for k in range(KB):
            there = hrecv.at[far, k]
            remote(there, there, bh_s.at[far, k], bh_r.at[far, k], half_peer).wait_recv()
            preact = ysum[far, k] + hrecv[far, k].astype(F32)
            hid[k, far, y] = jax.nn.gelu(preact, approximate=True).astype(BF16)
            mine = hid.at[k, far, y]
            gate("cy")
            for d in (2, 1, 3):
                start(remote(mine, mine, cy_s.at[far, k, d], cy_r.at[far, k, d], y_peer(d)), "cy")

    down_copy.wait()
    for k in range(KB):
        for far in range(2):
            for d in (1, 3, 2):
                there = hid.at[k, far, (y + NY - d) % NY]
                remote(there, there, cy_s.at[far, k, d], cy_r.at[far, k, d], y_peer(d)).wait_recv()
        hidden = hid[k].reshape(TOKENS, WB)
        rows = pl.ds(k * WB, WB)
        if k < KB - 1:
            hidden = dot(mix[...].reshape(TOKENS, TOKENS), hidden).astype(BF16)
            part = dot(hidden, down[rows, :]).reshape(p2.shape)
            p2[...] = part if k == 0 else part + p2[...]
        else:
            for core in (1 - c, c):
                mixed = dot(mix[:, core].reshape(HALF, TOKENS), hidden).astype(BF16)
                part = dot(mixed, down[rows, :])
                p2[:, core] = p2[:, core] + part.reshape(2, NX, SLAB, DM)
                if core is not c:
                    for far in (1, 0):
                        mine = p2.at[far, 1 - c]
                        start(remote(mine, crecv.at[far], dc_s.at[far], dc_r.at[far], core_peer))

    p_at = lax.broadcasted_iota(jnp.int32, (NX * 64, 2 * PART), 0)
    s_at = lax.broadcasted_iota(jnp.int32, (NX * 64, 2 * PART), 1)
    p_block = steps(p_at, 16, NX * 4)
    p_row = p_at - 16 * p_block
    one = s_at < PART
    two = s_at >= PART
    s_row = s_at - PART * jnp.where(two, 1, 0) - ROWS * p_block
    inside = (s_row >= 0) & (s_row < ROWS)
    put_main = onehot(inside & ((one & (s_row == p_row)) | (two & (s_row == p_row - 6))))
    put_middle = onehot(
        inside & ((one & (p_row < 14) & (s_row == p_row - 8)) | (two & (s_row == p_row - 14)))
    )
    put_middle = jnp.where(p_row >= 12, put_middle, 0)
    put_first = onehot(inside & (p_row >= 12) & (s_row == p_row - 12))[:, 0:PART]
    put_last = onehot(inside & (p_row >= 12) & (s_row == p_row - 10))[:, 0:PART]

    def pack(rows, to):
        main = dot(put_main, jnp.concatenate((rows[:, 0:640], rows[:, 640:1280]), axis=0))
        t10, t11 = rows[:, 1280:1408], rows[:, 1408:1536]
        tails = (
            dot(put_first, t10),
            dot(put_middle, jnp.concatenate((t10, t11), axis=0)),
            dot(put_last, t11),
        )
        for j in range(5):
            tile = main[:, j * 128 : (j + 1) * 128]
            if j < 3:
                tile = tile + tails[j]
            to[:, :, :, j * 128 : (j + 1) * 128] = tile.reshape(NX, 4, 16, 128).astype(to.dtype)

    rests = []
    order = ((7, 6, 5, 4), (3, 2, 1, 0))
    for far in (1, 0):
        mine = p2.at[far, 1 - c]
        remote(mine, crecv.at[far], dc_s.at[far], dc_r.at[far], core_peer).wait_recv()
        total = (p2[far, c] + crecv[far]).reshape(PART, DM)
        first = total.astype(BF16)
        pack(first, xsend.at[far])
        for step in order[1 - far]:
            for d in (2, 1, 3):
                mine = xsend.at[far, (x + d) % NX, z_at(step) % 4]
                start(remote(mine, xrecv.at[step, d], dx_s.at[step, d], dx_r.at[step, d], x_peer(d)))
        rests.append((far, (total - first.astype(F32)).astype(BF16)))
    for far, rest in rests:
        pack(rest, xown.at[far])
    for step in (*order[0], *order[1]):
        far, at = step // 4, z_at(step) % 4
        total = xown[far, x, at] + xsend[far, x, at].astype(F32)
        for d in (1, 3, 2):
            there = xrecv.at[step, d]
            remote(there, there, dx_s.at[step, d], dx_r.at[step, d], x_peer(d)).wait_recv()
            total = total + xrecv[step, d].astype(F32)
        if step:
            zsend[step] = total.astype(BF16)
            start(remote(zsend.at[step], zrecv.at[step], dz_s.at[step], dz_r.at[step], z_peer(step)))
    for step in (1, 2, 3, 4, 5, 6, 7):
        remote(zsend.at[step], zrecv.at[step], dz_s.at[step], dz_r.at[step], z_peer(step)).wait_recv()
        total = total + zrecv[step].astype(F32)
    for j in range(5):
        tile = total[:, j * 128 : (j + 1) * 128]
        out_ref[:, j * 128 : (j + 1) * 128] = tile[0:6].astype(BF16)
        out_ref[:, 640 + j * 128 : 768 + j * 128] = tile[6:12].astype(BF16)
    t10 = (total[12:16, 0:128], total[12:14, 128:256])
    t11 = (total[14:16, 128:256], total[12:16, 256:384])
    out_ref[:, 1280:1408] = jnp.concatenate(t10, axis=0).astype(BF16)
    out_ref[:, 1408:1536] = jnp.concatenate(t11, axis=0).astype(BF16)

    for chunks in ([sent], *flying.values()):
        for copies in chunks:
            for copy in copies:
                copy.wait_send()


def body(tokens, up_weight, down_weight, partner, spans):
    dma = pltpu.SemaphoreType.DMA
    vmem = pltpu.VMEM
    return pl.pallas_call(
        kernel,
        out_shape=jax.ShapeDtypeStruct((ROWS, DM), BF16),
        in_specs=[pl.BlockSpec(memory_space=pltpu.HBM)] * 5,
        out_specs=pl.BlockSpec(memory_space=vmem),
        scratch_shapes=[
            vmem((ROWS, DM), BF16),
            pltpu.SMEM((ROWS,), jnp.int32),
            pltpu.SMEM((1, 2), jnp.int32),
            vmem((DM, FF), BF16),
            vmem((FF, DM), BF16),
            vmem((2, NC, NX, NZ // 2, 16, 640), BF16),
            vmem((2, NC, PART, DM + 128), BF16),
            vmem((2, KB, NY, YR, WB), F32),
            vmem((2, NC, PART, TOKENS), BF16),
            vmem((2, KB, NY, YR, WB), BF16),
            vmem((2, KB, NY, YR, WB), BF16),
            vmem((2, KB, YR, WB), F32),
            vmem((2, KB, YR, WB), BF16),
            vmem((2, KB, YR, WB), BF16),
            vmem((KB, 2, NY, YR, WB), BF16),
            vmem((2, NC, NX, SLAB, DM), F32),
            vmem((2, NX, SLAB, DM), F32),
            vmem((2, NX, 4, 16, 640), BF16),
            vmem((NZ, NX, 16, 640), BF16),
            vmem((2, NX, 4, 16, 640), F32),
            vmem((NZ, 16, 640), BF16),
            vmem((NZ, 16, 640), BF16),
            dma((5,)),
            dma((NZ,)), dma((NZ,)),
            dma((NZ, NX)), dma((NZ, NX)),
            dma((2,)), dma((2,)),
            dma((2, KB, NY)), dma((2, KB, NY)),
            dma((2, KB)), dma((2, KB)),
            dma((2, KB, NY)), dma((2, KB, NY)),
            dma((2,)), dma((2,)),
            dma((NZ, NX)), dma((NZ, NX)),
            dma((NZ,)), dma((NZ,)),
        ],
        compiler_params=pltpu.CompilerParams(
            collective_id=0, has_side_effects=True, vmem_limit_bytes=60 << 20
        ),
    )(tokens, partner, spans, up_weight, down_weight)


def solution(mesh):
    placed = (
        P("wide", "narrow"),
        P("narrow", "wide"),
        P("wide", "narrow"),
        P("wide"),
        P("wide", None),
    )
    return jax.shard_map(
        body, mesh=mesh, in_specs=placed, out_specs=P("wide", "narrow"), check_vma=False
    )
```

```python
import jax
import jax.numpy as jnp
from jax import lax
from jax.experimental import pallas as pl
from jax.experimental.pallas import tpu as pltpu
from jax.sharding import PartitionSpec as P

MESH = pl.DeviceIdType.MESH
BF16 = jnp.bfloat16
F32 = jnp.float32

NZ, NX, NC, NY = 8, 4, 2, 4
ROWS = 6
SLAB = NZ // 2 * ROWS
PART = NX * SLAB
HALF = NC * PART
TOKENS = 2 * HALF
DM = 1536
FF = 768
GATED = {}
EARLY = 4
Z_SEND = (1, 2, 3, 4, 5, 6, 7)
KB = 3
WB = FF // KB
YR = HALF // NY


def steps(values, size, count):
    total = jnp.zeros_like(values)
    for k in range(1, count):
        total = total + jnp.where(values >= size * k, 1, 0)
    return total


def onehot(condition):
    return jnp.where(condition, 1.0, 0.0).astype(BF16)


def dot(a, b):
    return jnp.dot(a, b, preferred_element_type=F32)


def token_of(place, z_high):
    group = steps(place, SLAB, TOKENS // SLAB)
    inside = place - SLAB * group
    low = steps(inside, ROWS, NZ // 2)
    far = jnp.where(group >= NC * NX, 1, 0)
    core = jnp.where(group - NC * NX * far >= NX, 1, 0)
    column = group - NC * NX * far - NX * core
    z = (NZ // 2) * (z_high + far - 2 * z_high * far) + low
    block = (z * NX + column) * NC + core
    return block, ROWS * block + inside - ROWS * low


def kernel(
    tok_hbm, partner_hbm, spans_hbm, up_hbm, down_hbm, out_ref,
    tok_ref, partner_ref, spans_ref, up, down, planes, g, p1, mix, ysend, yrecv, ysum, hsend, hrecv, hid, p2,
    crecv, xsend, xrecv, xown, zsend, zrecv,
    wsem, az_s, az_r, ax_s, ax_r, ac_s, ac_r, by_s, by_r, bh_s, bh_r, cy_s, cy_r,
    dc_s, dc_r, dx_s, dx_r, dz_s, dz_r,
):
    w = lax.axis_index("wide")
    n = lax.axis_index("narrow")
    z, x, c = w // 8, (w // 2) % 4, w % 2
    half, y = n // 4, n % 4

    def z_at(step):
        bits = (z // 4, z // 2 % 2, z % 2)
        flip = (step // 4, step // 2 % 2, step % 2)
        high, middle, low = ((1 - b) if f else b for b, f in zip(bits, flip))
        return 4 * high + 2 * middle + low

    def z_peer(step):
        return ((z_at(step) * NX + x) * NC + c, n)

    def x_peer(d):
        return ((z * NX + (x + d) % NX) * NC + c, n)

    def y_peer(d):
        return (w, half * NY + (y + d) % NY)

    core_peer = ((z * NX + x) * NC + 1 - c, n)
    half_peer = (w, (1 - half) * NY + y)

    def remote(src, dst, send, recv, peer):
        return pltpu.make_async_remote_copy(
            src_ref=src, dst_ref=dst, send_sem=send, recv_sem=recv, device_id=peer, device_id_type=MESH
        )

    sent = []
    flying = {}

    def start(copy, phase=None):
        copy.start()
        if phase in GATED:
            flying[phase][-1].append(copy)
        else:
            sent.append(copy)

    def gate(phase):
        if phase in GATED:
            chunks = flying.setdefault(phase, [])
            if len(chunks) == GATED[phase]:
                for copy in chunks.pop(0):
                    copy.wait_send()
            chunks.append([])

    up_copy = pltpu.make_async_copy(up_hbm, up, wsem.at[0])
    down_copy = pltpu.make_async_copy(down_hbm, down, wsem.at[1])
    tok_copy = pltpu.make_async_copy(tok_hbm, tok_ref, wsem.at[2])
    partner_copy = pltpu.make_async_copy(partner_hbm, partner_ref, wsem.at[3])
    spans_copy = pltpu.make_async_copy(spans_hbm, spans_ref, wsem.at[4])
    tok_copy.start()
    partner_copy.start()
    spans_copy.start()
    up_copy.start()
    down_copy.start()

    barrier = pltpu.get_barrier_semaphore()
    peers = [half_peer]
    peers += [z_peer(d) for d in range(1, NZ)]
    peers += [y_peer(d) for d in range(1, NY)]
    peers += [x_peer(d) for d in range(1, NX)]
    peers += [core_peer]
    for peer in peers:
        pl.semaphore_signal(barrier, inc=1, device_id=peer, device_id_type=MESH)

    tok_copy.wait()
    partner_copy.wait()
    spans_copy.wait()
    tokens = tok_ref[...].astype(F32)
    row = lax.broadcasted_iota(jnp.int32, (ROWS, 128), 0)
    lane = lax.broadcasted_iota(jnp.int32, (ROWS, 128), 1)
    lower = jnp.full((ROWS, 128), spans_ref[0, 0], jnp.int32).astype(F32)
    upper = jnp.full((ROWS, 128), spans_ref[0, 1], jnp.int32).astype(F32)
    place = row.astype(F32)
    relative = jnp.zeros((ROWS, 128), F32)
    for r in range(ROWS):
        value = jnp.full((ROWS, 128), partner_ref[r] - ROWS * (w - 1), jnp.int32).astype(F32)
        relative = jnp.where(row == r, value, relative)
    share = jnp.where(lower > place, 0.5 * (lower - place) / lower, 0.0) + jnp.where(
        upper <= place, 0.5 * (place - upper + 1.0) / (ROWS - upper), 0.0
    )
    info = jnp.where(lane == 0, relative, jnp.where(lane == 1, share, 0.0))
    t10, t11 = tokens[:, 1280:1408], tokens[:, 1408:1536]
    tails = (
        (t10[0:4],),
        (t10[4:6], t11[0:2]),
        (t11[2:6],),
        (info[0:4],),
        (info[4:6], jnp.zeros((2, 128), F32)),
    )
    for j in range(5):
        main = (tokens[:, j * 128 : (j + 1) * 128], tokens[:, 640 + j * 128 : 768 + j * 128])
        tile = jnp.concatenate(main + tails[j], axis=0)
        planes[0, c, x, z % 4, :, j * 128 : (j + 1) * 128] = tile.astype(BF16)

    pl.semaphore_wait(barrier, len(peers))

    def plane(column, step):
        return planes.at[step // 4, c, column, z_at(step) % 4]

    for step in Z_SEND:
        there = planes.at[step // 4, c, x, z % 4]
        start(remote(plane(x, 0), there, az_s.at[step], az_r.at[step], z_peer(step)))

    def spread(step):
        mine = plane(x, step)
        if step:
            remote(mine, mine, az_s.at[step], az_r.at[step], z_peer(step)).wait_recv()
        for d in (2, 1, 3):
            start(remote(mine, mine, ax_s.at[step, d], ax_r.at[step, d], x_peer(d)))

    m_at = lax.broadcasted_iota(jnp.int32, (PART, PART * 16 // ROWS), 0)
    q_at = lax.broadcasted_iota(jnp.int32, (PART, PART * 16 // ROWS), 1)
    m_block = steps(m_at, ROWS, PART // ROWS)
    m_r = m_at - ROWS * m_block
    q_r = q_at - 16 * m_block
    picks = jnp.concatenate(
        (
            onehot(q_r == m_r),
            onehot(q_r == m_r + 6),
            onehot((m_r < 4) & (q_r == m_r + 12)),
            onehot((m_r >= 4) & (q_r == m_r + 8)),
            onehot((m_r < 2) & (q_r == m_r + 14)),
            onehot((m_r >= 2) & (q_r == m_r + 10)),
        ),
        axis=0,
    )

    def unpack(far):
        for d in (1, 3, 2):
            for step in range(4 * far, 4 * far + 4):
                there = plane((x + NX - d) % NX, step)
                remote(there, there, ax_s.at[step, d], ax_r.at[step, d], x_peer(d)).wait_recv()
        whole = planes[far, c].reshape(PART * 16 // ROWS, 640)
        low, high, first, second, third, fourth = dot(picks, whole).reshape(6, PART, 640)
        g[far, c, :, 0:640] = low.astype(BF16)
        g[far, c, :, 640:1280] = high.astype(BF16)
        g[far, c, :, 1280:1408] = (first[:, 0:128] + second[:, 128:256]).astype(BF16)
        g[far, c, :, 1408:1536] = (third[:, 128:256] + fourth[:, 256:384]).astype(BF16)
        g[far, c, :, 1536:1664] = (first[:, 384:512] + second[:, 512:640]).astype(BF16)
        mine = g.at[far, c]
        start(remote(mine, mine, ac_s.at[far], ac_r.at[far], core_peer))

    def project(far):
        there = g.at[far, 1 - c]
        remote(there, there, ac_s.at[far], ac_r.at[far], core_peer).wait_recv()
        a = g[far, :, :, 0:DM].reshape(HALF, DM)
        for k in range(KB):
            part = dot(a, up[:, k * WB : (k + 1) * WB]).reshape(NY, YR, WB)
            p1[far, k] = part
            ysend[far, k] = part.astype(BF16)
            gate("by")
            for d in (2, 1, 3):
                mine = ysend.at[far, k, (y + d) % NY]
                to = yrecv.at[far, k, d]
                start(remote(mine, to, by_s.at[far, k, d], by_r.at[far, k, d], y_peer(d)), "by")

    def exchange(far):
        for k in range(KB):
            total = p1[far, k, y]
            for d in (1, 3, 2):
                there = yrecv.at[far, k, d]
                remote(there, there, by_s.at[far, k, d], by_r.at[far, k, d], y_peer(d)).wait_recv()
                total = total + yrecv[far, k, d].astype(F32)
            ysum[far, k] = total
            hsend[far, k] = total.astype(BF16)
            gate("bh")
            mine = hsend.at[far, k]
            start(remote(mine, hrecv.at[far, k], bh_s.at[far, k], bh_r.at[far, k], half_peer), "bh")

    for step in range(EARLY):
        spread(step)
    unpack(0)
    for step in range(EARLY, NZ):
        spread(step)
    up_copy.wait()
    project(0)
    unpack(1)
    exchange(0)
    project(1)

    info = g[:, :, :, DM : DM + 128].reshape(TOKENS, 128).astype(F32)
    block, _ = token_of(lax.broadcasted_iota(jnp.int32, (TOKENS, 1), 0), z // 4)
    partner = (ROWS * (block - 1)).astype(F32) + info[:, 0:1]
    share = info[:, 1:2]
    _, token = token_of(lax.broadcasted_iota(jnp.int32, (1, TOKENS), 1), z // 4)
    at = lax.broadcasted_iota(jnp.int32, (TOKENS, TOKENS), 0)
    to = lax.broadcasted_iota(jnp.int32, (TOKENS, TOKENS), 1)
    matrix = jnp.where(at == to, 1.0 - share, 0.0) + jnp.where(token.astype(F32) == partner, share, 0.0)
    mix[...] = matrix.astype(BF16).reshape(mix.shape)

    exchange(1)
    for far in range(2):
        for k in range(KB):
            there = hrecv.at[far, k]
            remote(there, there, bh_s.at[far, k], bh_r.at[far, k], half_peer).wait_recv()
            preact = ysum[far, k] + hrecv[far, k].astype(F32)
            hid[k, far, y] = jax.nn.gelu(preact, approximate=True).astype(BF16)
            mine = hid.at[k, far, y]
            gate("cy")
            for d in (2, 1, 3):
                start(remote(mine, mine, cy_s.at[far, k, d], cy_r.at[far, k, d], y_peer(d)), "cy")

    down_copy.wait()
    for k in range(KB):
        for far in range(2):
            for d in (1, 3, 2):
                there = hid.at[k, far, (y + NY - d) % NY]
                remote(there, there, cy_s.at[far, k, d], cy_r.at[far, k, d], y_peer(d)).wait_recv()
        hidden = hid[k].reshape(TOKENS, WB)
        rows = pl.ds(k * WB, WB)
        if k < KB - 1:
            hidden = dot(mix[...].reshape(TOKENS, TOKENS), hidden).astype(BF16)
            part = dot(hidden, down[rows, :]).reshape(p2.shape)
            p2[...] = part if k == 0 else part + p2[...]
        else:
            for core, far in ((1 - c, 1), (1 - c, 0), (c, 1), (c, 0)):
                mixed = dot(mix[far, core], hidden).astype(BF16)
                part = dot(mixed, down[rows, :])
                p2[far, core] = p2[far, core] + part.reshape(NX, SLAB, DM)
                if core is not c:
                    mine = p2.at[far, 1 - c]
                    start(remote(mine, crecv.at[far], dc_s.at[far], dc_r.at[far], core_peer))

    p_at = lax.broadcasted_iota(jnp.int32, (NX * 64, 2 * PART), 0)
    s_at = lax.broadcasted_iota(jnp.int32, (NX * 64, 2 * PART), 1)
    p_block = steps(p_at, 16, NX * 4)
    p_row = p_at - 16 * p_block
    one = s_at < PART
    two = s_at >= PART
    s_row = s_at - PART * jnp.where(two, 1, 0) - ROWS * p_block
    inside = (s_row >= 0) & (s_row < ROWS)
    put_main = onehot(inside & ((one & (s_row == p_row)) | (two & (s_row == p_row - 6))))
    put_middle = onehot(
        inside & ((one & (p_row < 14) & (s_row == p_row - 8)) | (two & (s_row == p_row - 14)))
    )
    put_middle = jnp.where(p_row >= 12, put_middle, 0)
    put_first = onehot(inside & (p_row >= 12) & (s_row == p_row - 12))[:, 0:PART]
    put_last = onehot(inside & (p_row >= 12) & (s_row == p_row - 10))[:, 0:PART]

    def pack(rows, to):
        main = dot(put_main, jnp.concatenate((rows[:, 0:640], rows[:, 640:1280]), axis=0))
        t10, t11 = rows[:, 1280:1408], rows[:, 1408:1536]
        tails = (
            dot(put_first, t10),
            dot(put_middle, jnp.concatenate((t10, t11), axis=0)),
            dot(put_last, t11),
        )
        for j in range(5):
            tile = main[:, j * 128 : (j + 1) * 128]
            if j < 3:
                tile = tile + tails[j]
            to[:, :, :, j * 128 : (j + 1) * 128] = tile.reshape(NX, 4, 16, 128).astype(to.dtype)

    rests = []
    order = ((7, 6, 5, 4), (3, 2, 1, 0))
    for far in (1, 0):
        mine = p2.at[far, 1 - c]
        remote(mine, crecv.at[far], dc_s.at[far], dc_r.at[far], core_peer).wait_recv()
        total = (p2[far, c] + crecv[far]).reshape(PART, DM)
        first = total.astype(BF16)
        pack(first, xsend.at[far])
        for step in order[1 - far]:
            for d in (2, 1, 3):
                mine = xsend.at[far, (x + d) % NX, z_at(step) % 4]
                start(remote(mine, xrecv.at[step, d], dx_s.at[step, d], dx_r.at[step, d], x_peer(d)))
        rests.append((far, (total - first.astype(F32)).astype(BF16)))
    for far, rest in rests:
        pack(rest, xown.at[far])
    for step in (*order[0], *order[1]):
        far, at = step // 4, z_at(step) % 4
        total = xown[far, x, at] + xsend[far, x, at].astype(F32)
        for d in (1, 3, 2):
            there = xrecv.at[step, d]
            remote(there, there, dx_s.at[step, d], dx_r.at[step, d], x_peer(d)).wait_recv()
            total = total + xrecv[step, d].astype(F32)
        if step:
            zsend[step] = total.astype(BF16)
            start(remote(zsend.at[step], zrecv.at[step], dz_s.at[step], dz_r.at[step], z_peer(step)))
    for step in (1, 2, 3, 4, 5, 6, 7):
        remote(zsend.at[step], zrecv.at[step], dz_s.at[step], dz_r.at[step], z_peer(step)).wait_recv()
        total = total + zrecv[step].astype(F32)
    for j in range(5):
        tile = total[:, j * 128 : (j + 1) * 128]
        out_ref[:, j * 128 : (j + 1) * 128] = tile[0:6].astype(BF16)
        out_ref[:, 640 + j * 128 : 768 + j * 128] = tile[6:12].astype(BF16)
    t10 = (total[12:16, 0:128], total[12:14, 128:256])
    t11 = (total[14:16, 128:256], total[12:16, 256:384])
    out_ref[:, 1280:1408] = jnp.concatenate(t10, axis=0).astype(BF16)
    out_ref[:, 1408:1536] = jnp.concatenate(t11, axis=0).astype(BF16)

    for chunks in ([sent], *flying.values()):
        for copies in chunks:
            for copy in copies:
                copy.wait_send()


def body(tokens, up_weight, down_weight, partner, spans):
    dma = pltpu.SemaphoreType.DMA
    vmem = pltpu.VMEM
    return pl.pallas_call(
        kernel,
        out_shape=jax.ShapeDtypeStruct((ROWS, DM), BF16),
        in_specs=[pl.BlockSpec(memory_space=pltpu.HBM)] * 5,
        out_specs=pl.BlockSpec(memory_space=vmem),
        scratch_shapes=[
            vmem((ROWS, DM), BF16),
            pltpu.SMEM((ROWS,), jnp.int32),
            pltpu.SMEM((1, 2), jnp.int32),
            vmem((DM, FF), BF16),
            vmem((FF, DM), BF16),
            vmem((2, NC, NX, NZ // 2, 16, 640), BF16),
            vmem((2, NC, PART, DM + 128), BF16),
            vmem((2, KB, NY, YR, WB), F32),
            vmem((2, NC, PART, TOKENS), BF16),
            vmem((2, KB, NY, YR, WB), BF16),
            vmem((2, KB, NY, YR, WB), BF16),
            vmem((2, KB, YR, WB), F32),
            vmem((2, KB, YR, WB), BF16),
            vmem((2, KB, YR, WB), BF16),
            vmem((KB, 2, NY, YR, WB), BF16),
            vmem((2, NC, NX, SLAB, DM), F32),
            vmem((2, NX, SLAB, DM), F32),
            vmem((2, NX, 4, 16, 640), BF16),
            vmem((NZ, NX, 16, 640), BF16),
            vmem((2, NX, 4, 16, 640), F32),
            vmem((NZ, 16, 640), BF16),
            vmem((NZ, 16, 640), BF16),
            dma((5,)),
            dma((NZ,)), dma((NZ,)),
            dma((NZ, NX)), dma((NZ, NX)),
            dma((2,)), dma((2,)),
            dma((2, KB, NY)), dma((2, KB, NY)),
            dma((2, KB)), dma((2, KB)),
            dma((2, KB, NY)), dma((2, KB, NY)),
            dma((2,)), dma((2,)),
            dma((NZ, NX)), dma((NZ, NX)),
            dma((NZ,)), dma((NZ,)),
        ],
        compiler_params=pltpu.CompilerParams(
            collective_id=0, has_side_effects=True, vmem_limit_bytes=60 << 20
        ),
    )(tokens, partner, spans, up_weight, down_weight)


def solution(mesh):
    placed = (
        P("wide", "narrow"),
        P("narrow", "wide"),
        P("wide", "narrow"),
        P("wide"),
        P("wide", None),
    )
    return jax.shard_map(
        body, mesh=mesh, in_specs=placed, out_specs=P("wide", "narrow"), check_vma=False
    )
```
